512 devices in a mesh: seq: 64 (over x, z, core), tp: 8 (over y).
Axes of the slice: x: 4, y: 8, z: 8, core: 2. Of those that a mesh axis runs over, the one named last changes fastest.
Arguments:
- tokens: bfloat16 [16384, 4096], P('seq', 'tp'), may hold values from -6 to 6
- in_weight: bfloat16 [3, 4096, 2048], P(None, 'seq', 'tp'), may hold values from -0.09375 to 0.09375
- short_taps: float32 [3, 3, 2048], P(None, None, 'tp'), may hold values from -3.5 to 3.5
- long_filter: float32 [16384, 2048], P('seq', 'tp'), may hold values from -1.3 to 1.3
- skip: float32 [2048], P('tp'), may hold values from -4 to 4
- out_weight: bfloat16 [2048, 4096], P('tp'), may hold values from -0.125 to 0.125
Outputs:
- layer_out: bfloat16 [16384, 4096], P('seq', 'tp')
The draws below stay inside these ranges and needn't reach their ends.
All inputs are finite; a program needn't handle non-finite values.
Results may differ from the reference program's by a relative error of at most 0.0049.
Values may be sent and summed in bfloat16 or wider, within the bound.
No kernel may reach another device: no remote copies, remote signals or barrier semaphores. Data moves between devices by JAX's collectives and lax.ppermute only.
A program may use at most 64 MiB of HBM per device.

```python
import math
import jax
import jax.numpy as jnp

D = 4096
C = 2048
SHORT = 3
TOKENS = 16384


def draw_long_filter(key, part):
    key = jax.random.fold_in(key, 11)
    time_key, noise_key = jax.random.split(key, 2)
    lowest = math.log(20.0)
    times = jnp.exp(jax.random.uniform(time_key, (C,), jnp.float32, lowest, math.log(2.0 * TOKENS)))
    lags = jnp.arange(TOKENS, dtype=jnp.float32)[:, None]
    noise = jnp.clip(jax.random.normal(noise_key, (TOKENS, C), jnp.float32), -4.0, 4.0)
    scale = jnp.sqrt(2.0 / times)[None, :]
    return noise * scale * jnp.exp(-lags / times[None, :])


def block_scale(rng, shape, cuts, low, high):
    loudness, own = 1.0, jax.random.fold_in(rng, 6)
    for position, shards_of in cuts:
        heights = jnp.exp(jax.random.uniform(jax.random.fold_in(own, position), (shards_of,), jnp.float32, low / len(cuts), high / len(cuts)))
        loudness = loudness * jnp.repeat(heights, shape[position] // shards_of).reshape([-1 if axis == position else 1 for axis in range(len(shape))])
    return loudness


def normal_values(key, dims, width, bound, cuts=(), kind=jnp.bfloat16):
    loudness = block_scale(key, dims, cuts, -0.22, 0.18) if cuts else 1.0
    result = jax.random.normal(key, dims, jnp.float32) * width * loudness
    return jnp.minimum(jnp.maximum(result, -bound), bound).astype(kind)


def setup_inputs(seed: int = 0) -> dict:
    seeds = jax.random.split(jax.random.key(seed), 7)
    tokens = normal_values(seeds[0], (TOKENS, D), 1.0, 6.0, ((0, 64), (1, 8)))
    in_weight = normal_values(seeds[1], (3, D, C), D ** -0.5, 0.09375, ((1, 64), (2, 8)))
    short_taps = normal_values(seeds[2], (SHORT, 3, C), SHORT ** -0.5, 3.5, ((2, 8),), jnp.float32)
    long_filter = draw_long_filter(jax.random.fold_in(seeds[6], 71), 0)
    skip = normal_values(seeds[4], (C,), 1.0, 4.0, ((0, 8),), jnp.float32)
    out_weight = normal_values(seeds[5], (C, D), C ** -0.5, 0.125, ((0, 8),))
    return {"tokens": tokens, "in_weight": in_weight, "short_taps": short_taps, "long_filter": long_filter, "skip": skip, "out_weight": out_weight}


def reference(tokens, in_weight, short_taps, long_filter, skip, out_weight):
    projected = jnp.einsum('ld,bdc->blc', tokens.astype(jnp.float32), in_weight.astype(jnp.float32))
    rim_width = SHORT - 1
    padded = jnp.pad(projected, ((0, 0), (rim_width, 0), (0, 0)))
    mixed_branches = jnp.zeros_like(projected)
    for offset in range(SHORT):
        mixed_branches = mixed_branches + short_taps[offset][:, None, :] * padded[:, rim_width - offset: rim_width - offset + TOKENS, :]
    source = mixed_branches[1] * mixed_branches[0]
    length = 2 * TOKENS
    spectrum = jnp.fft.rfft(source, n=length, axis=0) * jnp.fft.rfft(long_filter, n=length, axis=0)
    long_conv = jnp.fft.irfft(spectrum, n=length, axis=0)[:TOKENS]
    gated_values = (mixed_branches[2] * (long_conv + skip[None, :] * source)).astype(jnp.bfloat16)
    return jnp.dot(gated_values, out_weight, preferred_element_type=jnp.float32).astype(jnp.bfloat16)
```

```python
import functools
import math

import jax
import jax.numpy as jnp
import ml_dtypes
import numpy as np
from jax import lax
from jax.experimental import pallas as pl
from jax.experimental.pallas import tpu as pltpu
from jax.sharding import PartitionSpec as P

SIDE = 128
BF = jnp.bfloat16


def split_table(table):
    high = table.astype(np.float32).astype(ml_dtypes.bfloat16)
    low = (table - high.astype(np.float64)).astype(np.float32).astype(ml_dtypes.bfloat16)
    return np.stack([high, low])


@functools.cache
def tables():
    length = 2 * SIDE * SIDE
    ids = np.arange(SIDE)
    first = 2 * math.pi * np.outer(ids + 0.5, ids) / (2 * SIDE)
    turn = 2 * math.pi * np.outer(ids + 0.5, ids) / length
    second = 2 * math.pi * (np.outer(ids, ids) % SIDE) / SIDE
    columns = np.concatenate([np.cos(first), -np.sin(first)], axis=0)
    cos_two, sin_two = np.cos(second), np.sin(second)
    forward = np.block([[cos_two, -sin_two], [sin_two, cos_two]])
    backward = np.block([[cos_two, sin_two], [-sin_two, cos_two]])
    twist = np.stack([np.cos(turn), np.sin(turn)]).astype(np.float32)
    return (
        split_table(columns),
        split_table(columns.T * (2.0 / length)),
        split_table(forward),
        split_table(backward),
        twist,
    )


def halves(value):
    high = value.astype(BF)
    return high, (value - high.astype(jnp.float32)).astype(BF)


def mm(left, right):
    return jnp.dot(left, right, preferred_element_type=jnp.float32)


def table_times(table, value):
    high, low = halves(value)
    return mm(table[0], high) + (mm(table[1], high) + mm(table[0], low))


def times_table(value, table):
    high, low = halves(value)
    return mm(high, table[0]) + (mm(high, table[1]) + mm(low, table[0]))


def spectrum(block, columns, forward, cosine, sine):
    first = table_times(columns, block)
    real, imag = first[:SIDE], first[SIDE:]
    turned = jnp.concatenate([real * cosine + imag * sine, imag * cosine - real * sine], axis=1)
    return times_table(turned, forward)


def filter_kernel(filter_ref, columns_ref, forward_ref, twist_ref, out_ref):
    columns = (columns_ref[0], columns_ref[1])
    forward = (forward_ref[0], forward_ref[1])
    for channel in range(filter_ref.shape[0]):
        out_ref[channel] = spectrum(
            filter_ref[channel], columns, forward, twist_ref[0], twist_ref[1]
        )


def conv_kernel(source_ref, spec_ref, columns_ref, rows_ref, forward_ref, backward_ref, twist_ref, out_ref):
    columns = (columns_ref[0], columns_ref[1])
    rows = (rows_ref[0], rows_ref[1])
    forward = (forward_ref[0], forward_ref[1])
    backward = (backward_ref[0], backward_ref[1])
    cosine, sine = twist_ref[0], twist_ref[1]
    for channel in range(source_ref.shape[0]):
        signal = spectrum(
            source_ref[channel].astype(jnp.float32), columns, forward, cosine, sine
        )
        sig_real, sig_imag = signal[:, :SIDE], signal[:, SIDE:]
        taps = spec_ref[channel]
        tap_real, tap_imag = taps[:, :SIDE], taps[:, SIDE:]
        product = jnp.concatenate(
            [sig_real * tap_real - sig_imag * tap_imag, sig_real * tap_imag + sig_imag * tap_real],
            axis=1,
        )
        back = times_table(product, backward)
        real, imag = back[:, :SIDE], back[:, SIDE:]
        turned = jnp.concatenate([real * cosine - imag * sine, imag * cosine + real * sine], axis=0)
        out_ref[channel] = table_times(rows, turned).astype(out_ref.dtype)


def filter_spectrum(blocks):
    columns, _, forward, _, twist = (jnp.asarray(table) for table in tables())
    count = blocks.shape[0]
    return pl.pallas_call(
        filter_kernel,
        out_shape=jax.ShapeDtypeStruct((count, SIDE, 2 * SIDE), jnp.float32),
        compiler_params=pltpu.CompilerParams(vmem_limit_bytes=16 * 2**20),
    )(blocks, columns, forward, twist)


def long_convolution(blocks, spec):
    columns, rows, forward, backward, twist = (jnp.asarray(table) for table in tables())
    return pl.pallas_call(
        conv_kernel,
        out_shape=jax.ShapeDtypeStruct(blocks.shape, BF),
        compiler_params=pltpu.CompilerParams(vmem_limit_bytes=16 * 2**20),
    )(blocks, spec, columns, rows, forward, backward, twist)


def body(groups, tokens, in_weight, short_taps, long_filter, skip, out_weight):
    x_groups, z_groups, core_groups, chip_groups = groups
    seq_count = lax.axis_size("seq")
    tp_count = lax.axis_size("tp")
    seq_index = lax.axis_index("seq")
    core = seq_index % 2
    chips = seq_count // 2
    rows = tokens.shape[0]
    depth = in_weight.shape[1]
    half = in_weight.shape[2] // 2
    own = half // chips

    def exchange(value, axis, members):
        return lax.all_to_all(
            value, axis, split_axis=0, concat_axis=0, tiled=True, axis_index_groups=members
        )

    def swap(value):
        return lax.ppermute(value, "seq", [(i, i ^ 1) for i in range(seq_count)])

    mine = lax.all_gather(tokens, "tp", axis=1, tiled=True)
    theirs = swap(mine)

    weights = in_weight.reshape(3, depth, 2, half).transpose(2, 1, 0, 3).reshape(2, depth, 3 * half)
    weights = exchange(weights, "seq", core_groups).reshape(1, 2 * depth, 3 * half)
    for members in (z_groups, x_groups):
        count = len(members[0])
        weights = exchange(
            jnp.broadcast_to(weights, (count,) + weights.shape[1:]), "seq", members
        ).reshape(1, -1, 3 * half)
    weights = weights[0]

    filter_in = long_filter.T.reshape(2, chips, own, rows).transpose(1, 0, 2, 3)
    filter_in = exchange(filter_in.reshape(seq_count, own, rows), "seq", None)
    filter_in = filter_in.transpose(1, 0, 2).reshape(own, SIDE, SIDE)
    spec = filter_spectrum(filter_in)

    piece = out_weight.shape[0] // seq_count
    out_columns = out_weight.shape[1] // tp_count
    wanted = lax.dynamic_slice_in_dim(out_weight, seq_index * piece, piece, 0)
    wanted = exchange(wanted.reshape(piece, tp_count, out_columns).transpose(1, 0, 2), "tp", None)
    wanted = lax.all_gather(wanted, "seq", axis=0)
    wanted = wanted.transpose(1, 0, 2, 3).reshape(-1, out_columns)

    def project(value):
        return jnp.dot(value, weights, preferred_element_type=jnp.float32)

    projected_mine, projected_theirs = project(mine), project(theirs)
    is_first = core == 0
    projected = jnp.concatenate(
        [
            jnp.where(is_first, projected_mine, projected_theirs),
            jnp.where(is_first, projected_theirs, projected_mine),
        ],
        axis=0,
    )
    chip_rows = 2 * rows
    rim = short_taps.shape[0] - 1
    before = lax.ppermute(
        projected[chip_rows - rim :], "seq", [(i, i + 2) for i in range(seq_count - 2)]
    )
    extended = jnp.concatenate([before, projected], axis=0)
    taps = lax.dynamic_slice_in_dim(short_taps, core * half, half, 2).reshape(rim + 1, 1, 3 * half)
    mixed = sum(
        taps[offset] * extended[rim - offset : rim - offset + chip_rows] for offset in range(rim + 1)
    )
    mixed = mixed.T.reshape(3, half, chip_rows)
    source = mixed[1] * mixed[0]

    blocks = exchange(source.astype(BF).reshape(chips, own, chip_rows), "seq", chip_groups)
    blocks = blocks.transpose(1, 0, 2).reshape(own, SIDE, SIDE)
    result = long_convolution(blocks, spec)
    result = result.reshape(own, chips, chip_rows).transpose(1, 0, 2)
    long_conv = exchange(result, "seq", chip_groups).reshape(half, chip_rows)

    own_skip = lax.dynamic_slice_in_dim(skip, core * half, half, 0)
    gated = (mixed[2] * (long_conv.astype(jnp.float32) + own_skip[:, None] * source)).astype(BF)
    gated = exchange(gated.reshape(half, 2, rows).transpose(1, 0, 2), "seq", core_groups)
    gated = gated.reshape(1, 2 * half, rows)
    gated = exchange(jnp.broadcast_to(gated, (tp_count,) + gated.shape[1:]), "tp", None)
    gated = gated.reshape(-1, rows)
    out = lax.dot_general(
        gated, wanted, (((0,), (0,)), ((), ())), preferred_element_type=jnp.float32
    )
    return out.astype(BF)


def solution(mesh):
    width, depth = 4, 8
    place = lambda x, z, c: (x * depth + z) * 2 + c
    x_groups = [[place(x, z, c) for x in range(width)] for z in range(depth) for c in range(2)]
    z_groups = [[place(x, z, c) for z in range(depth)] for x in range(width) for c in range(2)]
    core_groups = [[place(x, z, c) for c in range(2)] for x in range(width) for z in range(depth)]
    chip_groups = [
        [place(x, z, c) for x in range(width) for z in range(depth)] for c in range(2)
    ]
    return jax.shard_map(
        functools.partial(body, (x_groups, z_groups, core_groups, chip_groups)),
        mesh=mesh,
        in_specs=(
            P("seq", "tp"),
            P(None, "seq", "tp"),
            P(None, None, "tp"),
            P("seq", "tp"),
            P("tp"),
            P("tp", None),
        ),
        out_specs=P("seq", "tp"),
        check_vma=False,
    )
```

```python
import functools
import math

import jax
import jax.numpy as jnp
import ml_dtypes
import numpy as np
from jax import lax
from jax.experimental import pallas as pl
from jax.experimental.pallas import tpu as pltpu
from jax.sharding import PartitionSpec as P

SIDE = 128
BF = jnp.bfloat16


def split_table(table):
    high = table.astype(np.float32).astype(ml_dtypes.bfloat16)
    low = (table - high.astype(np.float64)).astype(np.float32).astype(ml_dtypes.bfloat16)
    return np.stack([high, low])


@functools.cache
def tables():
    length = 2 * SIDE * SIDE
    ids = np.arange(SIDE)
    first = 2 * math.pi * np.outer(ids + 0.5, ids) / (2 * SIDE)
    turn = 2 * math.pi * np.outer(ids + 0.5, ids) / length
    second = 2 * math.pi * (np.outer(ids, ids) % SIDE) / SIDE
    columns = np.concatenate([np.cos(first), -np.sin(first)], axis=0)
    cos_two, sin_two = np.cos(second), np.sin(second)
    forward = np.block([[cos_two, -sin_two], [sin_two, cos_two]])
    backward = np.block([[cos_two, sin_two], [-sin_two, cos_two]])
    twist = np.stack([np.cos(turn), np.sin(turn)]).astype(np.float32)
    return (
        split_table(columns),
        split_table(columns.T * (2.0 / length)),
        split_table(forward),
        split_table(backward),
        twist,
    )


def halves(value):
    high = value.astype(BF)
    return high, (value - high.astype(jnp.float32)).astype(BF)


def mm(left, right):
    return jnp.dot(left, right, preferred_element_type=jnp.float32)


def table_times(table, value):
    high, low = halves(value)
    return mm(table[0], high) + (mm(table[1], high) + mm(table[0], low))


def times_table(value, table):
    high, low = halves(value)
    return mm(high, table[0]) + (mm(high, table[1]) + mm(low, table[0]))


def spectrum(block, columns, forward, cosine, sine):
    first = table_times(columns, block)
    real, imag = first[:SIDE], first[SIDE:]
    turned = jnp.concatenate([real * cosine + imag * sine, imag * cosine - real * sine], axis=1)
    return times_table(turned, forward)


def filter_kernel(filter_ref, columns_ref, forward_ref, twist_ref, out_ref):
    columns = (columns_ref[0], columns_ref[1])
    forward = (forward_ref[0], forward_ref[1])
    for channel in range(filter_ref.shape[0]):
        out_ref[channel] = spectrum(
            filter_ref[channel], columns, forward, twist_ref[0], twist_ref[1]
        )


def conv_kernel(source_ref, spec_ref, columns_ref, rows_ref, forward_ref, backward_ref, twist_ref, out_ref):
    columns = (columns_ref[0], columns_ref[1])
    rows = (rows_ref[0], rows_ref[1])
    forward = (forward_ref[0], forward_ref[1])
    backward = (backward_ref[0], backward_ref[1])
    cosine, sine = twist_ref[0], twist_ref[1]
    for channel in range(source_ref.shape[0]):
        signal = spectrum(
            source_ref[channel].astype(jnp.float32), columns, forward, cosine, sine
        )
        sig_real, sig_imag = signal[:, :SIDE], signal[:, SIDE:]
        taps = spec_ref[channel]
        tap_real, tap_imag = taps[:, :SIDE], taps[:, SIDE:]
        product = jnp.concatenate(
            [sig_real * tap_real - sig_imag * tap_imag, sig_real * tap_imag + sig_imag * tap_real],
            axis=1,
        )
        back = times_table(product, backward)
        real, imag = back[:, :SIDE], back[:, SIDE:]
        turned = jnp.concatenate([real * cosine - imag * sine, imag * cosine + real * sine], axis=0)
        out_ref[channel] = table_times(rows, turned).astype(out_ref.dtype)


def filter_spectrum(blocks):
    columns, _, forward, _, twist = (jnp.asarray(table) for table in tables())
    count = blocks.shape[0]
    return pl.pallas_call(
        filter_kernel,
        out_shape=jax.ShapeDtypeStruct((count, SIDE, 2 * SIDE), jnp.float32),
        compiler_params=pltpu.CompilerParams(vmem_limit_bytes=16 * 2**20),
    )(blocks, columns, forward, twist)


def long_convolution(blocks, spec):
    columns, rows, forward, backward, twist = (jnp.asarray(table) for table in tables())
    return pl.pallas_call(
        conv_kernel,
        out_shape=jax.ShapeDtypeStruct(blocks.shape, BF),
        compiler_params=pltpu.CompilerParams(vmem_limit_bytes=16 * 2**20),
    )(blocks, spec, columns, rows, forward, backward, twist)


def body(groups, tokens, in_weight, short_taps, long_filter, skip, out_weight):
    x_groups, zc_groups, chip_groups, column_groups = groups
    seq_count = lax.axis_size("seq")
    tp_count = lax.axis_size("tp")
    seq_index = lax.axis_index("seq")
    tp_index = lax.axis_index("tp")
    core = seq_index % 2
    chips = seq_count // 2
    rows = tokens.shape[0]
    chip_rows = 2 * rows
    depth = in_weight.shape[1]
    width = in_weight.shape[2]
    half = width // 2
    own = half // chips
    features = tokens.shape[1]

    def exchange(value, axis, members):
        return lax.all_to_all(
            value, axis, split_axis=0, concat_axis=0, tiled=True, axis_index_groups=members
        )

    def swap(value):
        return lax.ppermute(value, "seq", [(i, i ^ 1) for i in range(seq_count)])

    members = len(zc_groups[0])
    piece = out_weight.shape[0] // members
    strip = lax.dynamic_slice_in_dim(out_weight, (seq_index % members) * piece, piece, 0)
    strip = strip.reshape(piece, tp_count, features).transpose(1, 0, 2).reshape(-1, features)
    mine = lax.all_gather(jnp.concatenate([tokens, strip], axis=0), "tp", axis=1, tiled=True)

    weights = in_weight.reshape(3, depth, 2, half).transpose(2, 1, 0, 3)
    weights = weights.reshape(1, 2, depth, 3 * half)
    weights = exchange(
        jnp.broadcast_to(weights, (members // 2, 2, depth, 3 * half)).reshape(-1, depth, 3 * half),
        "seq",
        zc_groups,
    ).reshape(-1, 3 * half)
    late_weights = lax.all_gather(
        weights[:, width:], "seq", axis=0, tiled=True, axis_index_groups=x_groups
    )
    count = len(x_groups[0])
    weights = jnp.broadcast_to(weights[None, :, :width], (count, weights.shape[0], width))
    weights = exchange(weights, "seq", x_groups).reshape(-1, width)
    mine, weights = lax.optimization_barrier((mine, weights))
    theirs = swap(mine)

    filter_in = long_filter.T.reshape(2, chips, own, rows).transpose(1, 0, 2, 3)
    filter_in = exchange(filter_in.reshape(seq_count, own, rows), "seq", None)
    filter_in = filter_in.transpose(1, 0, 2).reshape(own, SIDE, SIDE)
    spec = filter_spectrum(filter_in)

    rim = short_taps.shape[0] - 1
    is_first = core == 0
    own_taps = lax.dynamic_slice_in_dim(short_taps, core * half, half, 2)

    def project(mine, table, taps):
        first = jnp.dot(mine, table, preferred_element_type=jnp.float32)[:rows]
        second = jnp.dot(theirs, table, preferred_element_type=jnp.float32)[:rows]
        upper = jnp.where(is_first, first, second)
        lower = jnp.where(is_first, second, first)
        before = lax.ppermute(
            lower[rows - rim :], "seq", [(i, i + 2) for i in range(seq_count - 2)]
        )
        extended = jnp.concatenate([before, upper, lower], axis=0)
        return sum(
            taps[offset] * extended[rim - offset : rim - offset + chip_rows]
            for offset in range(rim + 1)
        )

    early = project(mine, weights, own_taps[:, :2].reshape(rim + 1, 1, width)).T
    source = early[half:] * early[:half]

    sent = source.astype(BF).reshape(chips, own, chip_rows)
    sent, spec = lax.optimization_barrier((sent, spec))
    later, _ = lax.optimization_barrier((mine, sent))
    blocks = exchange(sent, "seq", chip_groups)
    blocks = blocks.transpose(1, 0, 2).reshape(own, SIDE, SIDE)
    result = long_convolution(blocks, spec)
    result = result.reshape(own, chips, chip_rows).transpose(1, 0, 2)
    long_conv = exchange(result, "seq", chip_groups).reshape(half, chip_rows)

    strip = lax.dynamic_slice_in_dim(later, rows + tp_index * piece, piece, 0)
    wanted = lax.all_gather(
        strip.reshape(piece, tp_count, features), "seq", axis=0, axis_index_groups=zc_groups
    )
    wanted = wanted.transpose(2, 0, 1, 3).reshape(-1, features)

    gate = project(later, late_weights, own_taps[:, 2].reshape(rim + 1, 1, half)).T
    own_skip = lax.dynamic_slice_in_dim(skip, core * half, half, 0)
    gated = (gate * (long_conv.astype(jnp.float32) + own_skip[:, None] * source)).astype(BF)
    gated = gated.reshape(half, 2, rows).transpose(1, 0, 2)
    gated = jnp.broadcast_to(gated, (tp_count,) + gated.shape).reshape(-1, half, rows)
    gated = exchange(gated, ("seq", "tp"), column_groups).reshape(-1, rows)
    out = lax.dot_general(
        gated, wanted, (((0,), (0,)), ((), ())), preferred_element_type=jnp.float32
    )
    return out.astype(BF)


def solution(mesh):
    width, depth, tp = 4, 8, mesh.shape["tp"]
    place = lambda x, z, c: (x * depth + z) * 2 + c
    chips = [(x, z) for x in range(width) for z in range(depth)]
    x_groups = [[place(x, z, c) for x in range(width)] for z in range(depth) for c in range(2)]
    zc_groups = [[place(x, z, c) for z in range(depth) for c in range(2)] for x in range(width)]
    chip_groups = [[place(x, z, c) for x, z in chips] for c in range(2)]
    column_groups = [
        [place(x, z, c) * tp + y for y in range(tp) for c in range(2)] for x, z in chips
    ]
    return jax.shard_map(
        functools.partial(body, (x_groups, zc_groups, chip_groups, column_groups)),
        mesh=mesh,
        in_specs=(
            P("seq", "tp"),
            P(None, "seq", "tp"),
            P(None, None, "tp"),
            P("seq", "tp"),
            P("tp"),
            P("tp", None),
        ),
        out_specs=P("seq", "tp"),
        check_vma=False,
    )
```

```python
import functools
import math

import jax
import jax.numpy as jnp
import ml_dtypes
import numpy as np
from jax import lax
from jax.experimental import pallas as pl
from jax.experimental.pallas import tpu as pltpu
from jax.sharding import PartitionSpec as P

SIDE = 128
BF = jnp.bfloat16


def split_table(table):
    high = table.astype(np.float32).astype(ml_dtypes.bfloat16)
    low = (table - high.astype(np.float64)).astype(np.float32).astype(ml_dtypes.bfloat16)
    return np.stack([high, low])


@functools.cache
def tables():
    length = 2 * SIDE * SIDE
    ids = np.arange(SIDE)
    first = 2 * math.pi * np.outer(ids + 0.5, ids) / (2 * SIDE)
    turn = 2 * math.pi * np.outer(ids + 0.5, ids) / length
    second = 2 * math.pi * (np.outer(ids, ids) % SIDE) / SIDE
    columns = np.concatenate([np.cos(first), -np.sin(first)], axis=0)
    cos_two, sin_two = np.cos(second), np.sin(second)
    forward = np.block([[cos_two, -sin_two], [sin_two, cos_two]])
    backward = np.block([[cos_two, sin_two], [-sin_two, cos_two]])
    twist = np.stack([np.cos(turn), np.sin(turn)]).astype(np.float32)
    return (
        split_table(columns),
        split_table(columns.T * (2.0 / length)),
        split_table(forward),
        split_table(backward),
        twist,
    )


def halves(value):
    high = value.astype(BF)
    return high, (value - high.astype(jnp.float32)).astype(BF)


def mm(left, right):
    return jnp.dot(left, right, preferred_element_type=jnp.float32)


def table_times(table, value):
    high, low = halves(value)
    return mm(table[0], high) + (mm(table[1], high) + mm(table[0], low))


def times_table(value, table):
    high, low = halves(value)
    return mm(high, table[0]) + (mm(high, table[1]) + mm(low, table[0]))


def spectrum(block, columns, forward, cosine, sine):
    first = table_times(columns, block)
    real, imag = first[:SIDE], first[SIDE:]
    turned = jnp.concatenate([real * cosine + imag * sine, imag * cosine - real * sine], axis=1)
    return times_table(turned, forward)


def filter_kernel(filter_ref, columns_ref, forward_ref, twist_ref, out_ref):
    columns = (columns_ref[0], columns_ref[1])
    forward = (forward_ref[0], forward_ref[1])
    for channel in range(filter_ref.shape[0]):
        out_ref[channel] = spectrum(
            filter_ref[channel], columns, forward, twist_ref[0], twist_ref[1]
        )


def conv_kernel(source_ref, spec_ref, columns_ref, rows_ref, forward_ref, backward_ref, twist_ref, out_ref):
    columns = (columns_ref[0], columns_ref[1])
    rows = (rows_ref[0], rows_ref[1])
    forward = (forward_ref[0], forward_ref[1])
    backward = (backward_ref[0], backward_ref[1])
    cosine, sine = twist_ref[0], twist_ref[1]
    for channel in range(source_ref.shape[0]):
        signal = spectrum(
            source_ref[channel].astype(jnp.float32), columns, forward, cosine, sine
        )
        sig_real, sig_imag = signal[:, :SIDE], signal[:, SIDE:]
        taps = spec_ref[channel]
        tap_real, tap_imag = taps[:, :SIDE], taps[:, SIDE:]
        product = jnp.concatenate(
            [sig_real * tap_real - sig_imag * tap_imag, sig_real * tap_imag + sig_imag * tap_real],
            axis=1,
        )
        back = times_table(product, backward)
        real, imag = back[:, :SIDE], back[:, SIDE:]
        turned = jnp.concatenate([real * cosine - imag * sine, imag * cosine + real * sine], axis=0)
        out_ref[channel] = table_times(rows, turned).astype(out_ref.dtype)


def filter_spectrum(blocks):
    columns, _, forward, _, twist = (jnp.asarray(table) for table in tables())
    count = blocks.shape[0]
    return pl.pallas_call(
        filter_kernel,
        out_shape=jax.ShapeDtypeStruct((count, SIDE, 2 * SIDE), jnp.float32),
        compiler_params=pltpu.CompilerParams(vmem_limit_bytes=16 * 2**20),
    )(blocks, columns, forward, twist)


def long_convolution(blocks, spec):
    columns, rows, forward, backward, twist = (jnp.asarray(table) for table in tables())
    return pl.pallas_call(
        conv_kernel,
        out_shape=jax.ShapeDtypeStruct(blocks.shape, BF),
        compiler_params=pltpu.CompilerParams(vmem_limit_bytes=16 * 2**20),
    )(blocks, spec, columns, rows, forward, backward, twist)


def product_kernel(side_ref, left_ref, right_ref, out_ref, total_ref):
    step = pl.program_id(0)
    table = right_ref[...].reshape(left_ref.shape[0], right_ref.shape[-1])
    part = lax.dot_general(
        left_ref[...], table, (((0,), (0,)), ((), ())), preferred_element_type=jnp.float32
    )

    @pl.when(step == 0)
    def _():
        total_ref[...] = part

    @pl.when(step > 0)
    def _():
        total_ref[...] += part

    @pl.when(step == pl.num_programs(0) - 1)
    def _():
        out_ref[...] = total_ref[...].astype(out_ref.dtype)


def product(left, right, side, steps):
    members, piece, columns = right.shape
    piece //= 2
    columns //= steps
    block = members * piece
    rows = left.shape[1]
    return pl.pallas_call(
        product_kernel,
        grid_spec=pltpu.PrefetchScalarGridSpec(
            num_scalar_prefetch=1,
            grid=(steps,),
            in_specs=[
                pl.BlockSpec((block, rows), lambda k, side: (k, 0)),
                pl.BlockSpec((members, piece, columns), lambda k, side: (0, side[0], k)),
            ],
            out_specs=pl.BlockSpec((rows, columns), lambda k, side: (0, 0)),
            scratch_shapes=[pltpu.VMEM((rows, columns), jnp.float32)],
        ),
        out_shape=jax.ShapeDtypeStruct((rows, columns), BF),
        cost_estimate=pl.CostEstimate(
            flops=2 * rows * steps * block * columns,
            bytes_accessed=2 * steps * block * (rows + columns),
            transcendentals=0,
        ),
        compiler_params=pltpu.CompilerParams(vmem_limit_bytes=16 * 2**20),
    )(side.reshape(1), left, right)


def body(groups, tokens, in_weight, short_taps, long_filter, skip, out_weight):
    x_groups, zc_groups, chip_groups, column_groups = groups
    seq_count = lax.axis_size("seq")
    tp_count = lax.axis_size("tp")
    seq_index = lax.axis_index("seq")
    tp_index = lax.axis_index("tp")
    core = seq_index % 2
    chips = seq_count // 2
    rows = tokens.shape[0]
    chip_rows = 2 * rows
    depth = in_weight.shape[1]
    width = in_weight.shape[2]
    half = width // 2
    own = half // chips
    features = tokens.shape[1]

    def exchange(value, axis, members):
        return lax.all_to_all(
            value, axis, split_axis=0, concat_axis=0, tiled=True, axis_index_groups=members
        )

    def swap(value):
        return lax.ppermute(value, "seq", [(i, i ^ 1) for i in range(seq_count)])

    members = len(zc_groups[0])
    piece = out_weight.shape[0] // members
    strip = lax.dynamic_slice_in_dim(out_weight, (seq_index % members) * piece, piece, 0)
    strip = strip.reshape(piece, tp_count, features).transpose(1, 0, 2).reshape(-1, features)
    mine = lax.all_gather(jnp.concatenate([tokens, strip], axis=0), "tp", axis=1, tiled=True)

    weights = in_weight.reshape(3, depth, 2, half).transpose(2, 1, 0, 3)
    weights = weights.reshape(1, 2, depth, 3 * half)
    weights = exchange(
        jnp.broadcast_to(weights, (members // 2, 2, depth, 3 * half)).reshape(-1, depth, 3 * half),
        "seq",
        zc_groups,
    ).reshape(-1, 3 * half)
    late_weights = lax.all_gather(
        weights[:, width:], "seq", axis=0, tiled=True, axis_index_groups=x_groups
    )
    count = len(x_groups[0])
    weights = jnp.broadcast_to(weights[None, :, :width], (count, weights.shape[0], width))
    weights = exchange(weights, "seq", x_groups).reshape(-1, width)
    mine, weights = lax.optimization_barrier((mine, weights))
    theirs = swap(mine)

    filter_in = long_filter.T.reshape(2, chips, own, rows).transpose(1, 0, 2, 3)
    filter_in = exchange(filter_in.reshape(seq_count, own, rows), "seq", None)
    filter_in = filter_in.transpose(1, 0, 2).reshape(own, SIDE, SIDE)
    rim = short_taps.shape[0] - 1
    is_first = core == 0
    own_taps = lax.dynamic_slice_in_dim(short_taps, core * half, half, 2)

    def project(mine, table, taps):
        first = jnp.dot(mine, table, preferred_element_type=jnp.float32)[:rows]
        second = jnp.dot(theirs, table, preferred_element_type=jnp.float32)[:rows]
        upper = jnp.where(is_first, first, second)
        lower = jnp.where(is_first, second, first)
        before = lax.ppermute(
            lower[rows - rim :], "seq", [(i, i + 2) for i in range(seq_count - 2)]
        )
        extended = jnp.concatenate([before, upper, lower], axis=0)
        return sum(
            taps[offset] * extended[rim - offset : rim - offset + chip_rows]
            for offset in range(rim + 1)
        )

    early = project(mine, weights, own_taps[:, :2].reshape(rim + 1, 1, width)).T
    source = early[half:] * early[:half]

    sent = source.astype(BF).reshape(chips, own, chip_rows)
    sent, filter_in = lax.optimization_barrier((sent, filter_in))
    later, _ = lax.optimization_barrier((mine, sent))
    blocks = exchange(sent, "seq", chip_groups)
    blocks = blocks.transpose(1, 0, 2).reshape(own, SIDE, SIDE)
    result = long_convolution(blocks, filter_spectrum(filter_in))
    result = result.reshape(own, chips, chip_rows).transpose(1, 0, 2)
    long_conv = exchange(result, "seq", chip_groups).reshape(half, chip_rows)

    pair_piece = 2 * piece
    strip = lax.dynamic_slice_in_dim(
        later, rows + (tp_index // 2) * pair_piece, pair_piece, 0
    )
    wanted = lax.all_gather(
        strip, "seq", axis=0, axis_index_groups=zc_groups
    )

    gate = project(later, late_weights, own_taps[:, 2].reshape(rim + 1, 1, half)).T
    own_skip = lax.dynamic_slice_in_dim(skip, core * half, half, 0)
    gated = (gate * (long_conv.astype(jnp.float32) + own_skip[:, None] * source)).astype(BF)
    quarter = rows // 2
    gated = gated.reshape(half, 2, 2, quarter).transpose(2, 1, 0, 3)
    gated = jnp.broadcast_to(gated, (tp_count // 2,) + gated.shape).reshape(-1, half, quarter)
    gated = exchange(gated, ("seq", "tp"), column_groups).reshape(-1, quarter)
    side = tp_index % 2
    given = product(gated, wanted, 1 - side, tp_count)
    given = lax.ppermute(given, "tp", [(i, i ^ 1) for i in range(tp_count)])
    kept = product(gated, wanted, side, tp_count)
    is_even = side == 0
    return jnp.concatenate(
        [jnp.where(is_even, kept, given), jnp.where(is_even, given, kept)], axis=0
    )


def solution(mesh):
    width, depth, tp = 4, 8, mesh.shape["tp"]
    place = lambda x, z, c: (x * depth + z) * 2 + c
    chips = [(x, z) for x in range(width) for z in range(depth)]
    x_groups = [[place(x, z, c) for x in range(width)] for z in range(depth) for c in range(2)]
    zc_groups = [[place(x, z, c) for z in range(depth) for c in range(2)] for x in range(width)]
    chip_groups = [[place(x, z, c) for x, z in chips] for c in range(2)]
    column_groups = [
        [place(x, z, c) * tp + y for y in range(tp) for c in range(2)] for x, z in chips
    ]
    return jax.shard_map(
        functools.partial(body, (x_groups, zc_groups, chip_groups, column_groups)),
        mesh=mesh,
        in_specs=(
            P("seq", "tp"),
            P(None, "seq", "tp"),
            P(None, None, "tp"),
            P("seq", "tp"),
            P("tp"),
            P("tp", None),
        ),
        out_specs=P("seq", "tp"),
        check_vma=False,
    )
```

```python
import functools
import math

import jax
import jax.numpy as jnp
import ml_dtypes
import numpy as np
from jax import lax
from jax.experimental import pallas as pl
from jax.experimental.pallas import tpu as pltpu
from jax.sharding import PartitionSpec as P

SIDE = 128
BF = jnp.bfloat16


def split_table(table):
    high = table.astype(np.float32).astype(ml_dtypes.bfloat16)
    low = (table - high.astype(np.float64)).astype(np.float32).astype(ml_dtypes.bfloat16)
    return np.stack([high, low])


@functools.cache
def tables():
    length = 2 * SIDE * SIDE
    ids = np.arange(SIDE)
    first = 2 * math.pi * np.outer(ids + 0.5, ids) / (2 * SIDE)
    turn = 2 * math.pi * np.outer(ids + 0.5, ids) / length
    second = 2 * math.pi * (np.outer(ids, ids) % SIDE) / SIDE
    columns = np.concatenate([np.cos(first), -np.sin(first)], axis=0)
    cos_two, sin_two = np.cos(second), np.sin(second)
    forward = np.block([[cos_two, -sin_two], [sin_two, cos_two]])
    backward = np.block([[cos_two, sin_two], [-sin_two, cos_two]])
    twist = np.stack([np.cos(turn), np.sin(turn)]).astype(np.float32)
    return (
        split_table(columns),
        split_table(columns.T * (2.0 / length)),
        split_table(forward),
        split_table(backward),
        twist,
    )


def halves(value):
    high = value.astype(BF)
    return high, (value - high.astype(jnp.float32)).astype(BF)


def mm(left, right):
    return jnp.dot(left, right, preferred_element_type=jnp.float32)


def table_times(table, value):
    high, low = halves(value)
    return mm(table[0], high) + (mm(table[1], high) + mm(table[0], low))


def times_table(value, table):
    high, low = halves(value)
    return mm(high, table[0]) + (mm(high, table[1]) + mm(low, table[0]))


def spectrum(block, columns, forward, cosine, sine):
    first = table_times(columns, block)
    real, imag = first[:SIDE], first[SIDE:]
    turned = jnp.concatenate([real * cosine + imag * sine, imag * cosine - real * sine], axis=1)
    return times_table(turned, forward)


def filter_kernel(filter_ref, columns_ref, forward_ref, twist_ref, out_ref):
    columns = (columns_ref[0], columns_ref[1])
    forward = (forward_ref[0], forward_ref[1])
    for channel in range(filter_ref.shape[0]):
        out_ref[channel] = spectrum(
            filter_ref[channel], columns, forward, twist_ref[0], twist_ref[1]
        )


def conv_kernel(source_ref, spec_ref, columns_ref, rows_ref, forward_ref, backward_ref, twist_ref, out_ref):
    columns = (columns_ref[0], columns_ref[1])
    rows = (rows_ref[0], rows_ref[1])
    forward = (forward_ref[0], forward_ref[1])
    backward = (backward_ref[0], backward_ref[1])
    cosine, sine = twist_ref[0], twist_ref[1]
    _, chips, chip_rows = source_ref.shape
    starts = range(0, chip_rows, SIDE)
    for channel in range(source_ref.shape[0]):
        signal = spectrum(
            jnp.concatenate(
                [source_ref[channel, :, start : start + SIDE] for start in starts], axis=0
            ).astype(jnp.float32),
            columns, forward, cosine, sine,
        )
        sig_real, sig_imag = signal[:, :SIDE], signal[:, SIDE:]
        taps = spec_ref[channel]
        tap_real, tap_imag = taps[:, :SIDE], taps[:, SIDE:]
        product = jnp.concatenate(
            [sig_real * tap_real - sig_imag * tap_imag, sig_real * tap_imag + sig_imag * tap_real],
            axis=1,
        )
        back = times_table(product, backward)
        real, imag = back[:, :SIDE], back[:, SIDE:]
        turned = jnp.concatenate([real * cosine - imag * sine, imag * cosine + real * sine], axis=0)
        result = table_times(rows, turned).astype(out_ref.dtype)
        for index, start in enumerate(starts):
            out_ref[channel, :, start : start + SIDE] = result[index * chips : (index + 1) * chips]


def filter_spectrum(blocks):
    columns, _, forward, _, twist = (jnp.asarray(table) for table in tables())
    count = blocks.shape[0]
    return pl.pallas_call(
        filter_kernel,
        out_shape=jax.ShapeDtypeStruct((count, SIDE, 2 * SIDE), jnp.float32),
        compiler_params=pltpu.CompilerParams(vmem_limit_bytes=16 * 2**20),
    )(blocks, columns, forward, twist)


def long_convolution(blocks, spec):
    columns, rows, forward, backward, twist = tables()
    chips, parts = blocks.shape[1], blocks.shape[2] // SIDE
    order = (np.arange(chips)[None, :] * parts + np.arange(parts)[:, None]).reshape(-1)
    columns, rows = columns[:, :, order], rows[:, order, :]
    columns, rows, forward, backward, twist = (
        jnp.asarray(table) for table in (columns, rows, forward, backward, twist)
    )
    return pl.pallas_call(
        conv_kernel,
        out_shape=jax.ShapeDtypeStruct(blocks.shape, BF),
        compiler_params=pltpu.CompilerParams(vmem_limit_bytes=16 * 2**20),
    )(blocks, spec, columns, rows, forward, backward, twist)


def body(groups, tokens, in_weight, short_taps, long_filter, skip, out_weight):
    x_groups, zc_groups, chip_groups, column_groups = groups
    seq_count = lax.axis_size("seq")
    tp_count = lax.axis_size("tp")
    seq_index = lax.axis_index("seq")
    tp_index = lax.axis_index("tp")
    core = seq_index % 2
    chips = seq_count // 2
    rows = tokens.shape[0]
    chip_rows = 2 * rows
    depth = in_weight.shape[1]
    width = in_weight.shape[2]
    half = width // 2
    own = half // chips
    features = tokens.shape[1]

    def exchange(value, axis, members):
        return lax.all_to_all(
            value, axis, split_axis=0, concat_axis=0, tiled=True, axis_index_groups=members
        )

    def swap(value):
        return lax.ppermute(value, "seq", [(i, i ^ 1) for i in range(seq_count)])

    members = len(zc_groups[0])
    piece = out_weight.shape[0] // members
    strip = lax.dynamic_slice_in_dim(out_weight, (seq_index % members) * piece, piece, 0)
    strip = strip.reshape(piece, tp_count, features).transpose(1, 0, 2).reshape(-1, features)
    mine = lax.all_gather(jnp.concatenate([tokens, strip], axis=0), "tp", axis=1, tiled=True)

    weights = in_weight.reshape(3, depth, 2, half).transpose(2, 1, 0, 3)
    weights = weights.reshape(1, 2, depth, 3 * half)
    weights = exchange(
        jnp.broadcast_to(weights, (members // 2, 2, depth, 3 * half)).reshape(-1, depth, 3 * half),
        "seq",
        zc_groups,
    ).reshape(-1, 3 * half)
    late_weights = lax.all_gather(
        weights[:, width:], "seq", axis=0, tiled=True, axis_index_groups=x_groups
    )
    count = len(x_groups[0])
    weights = jnp.broadcast_to(weights[None, :, :width], (count, weights.shape[0], width))
    weights = exchange(weights, "seq", x_groups).reshape(-1, width)
    mine, weights = lax.optimization_barrier((mine, weights))
    theirs = swap(mine)

    filter_in = long_filter.T.reshape(2, chips, own, rows).transpose(1, 0, 2, 3)
    filter_in = exchange(filter_in.reshape(seq_count, own, rows), "seq", None)
    filter_in = filter_in.transpose(1, 0, 2).reshape(own, SIDE, SIDE)
    spec = filter_spectrum(filter_in)

    rim = short_taps.shape[0] - 1
    is_first = core == 0
    own_taps = lax.dynamic_slice_in_dim(short_taps, core * half, half, 2)

    def project(mine, table, taps):
        first = jnp.dot(mine, table, preferred_element_type=jnp.float32)[:rows]
        second = jnp.dot(theirs, table, preferred_element_type=jnp.float32)[:rows]
        upper = jnp.where(is_first, first, second)
        lower = jnp.where(is_first, second, first)
        before = lax.ppermute(
            lower[rows - rim :], "seq", [(i, i + 2) for i in range(seq_count - 2)]
        )
        extended = jnp.concatenate([before, upper, lower], axis=0)
        return sum(
            taps[offset] * extended[rim - offset : rim - offset + chip_rows]
            for offset in range(rim + 1)
        )

    early = project(mine, weights, own_taps[:, :2].reshape(rim + 1, 1, width)).T
    source = early[half:] * early[:half]

    sent = source.astype(BF).reshape(chips, own, chip_rows)
    sent, spec = lax.optimization_barrier((sent, spec))
    later, _ = lax.optimization_barrier((mine, sent))
    blocks = exchange(sent, "seq", chip_groups)
    blocks = blocks.transpose(1, 0, 2)
    result = long_convolution(blocks, spec)
    result = result.transpose(1, 0, 2)
    long_conv = exchange(result, "seq", chip_groups).reshape(half, chip_rows)

    strip = lax.dynamic_slice_in_dim(later, rows + tp_index * piece, piece, 0)
    wanted = lax.all_gather(
        strip.reshape(piece, tp_count, features), "seq", axis=0, axis_index_groups=zc_groups
    )
    wanted = wanted.transpose(2, 0, 1, 3).reshape(-1, features)

    gate = project(later, late_weights, own_taps[:, 2].reshape(rim + 1, 1, half)).T
    own_skip = lax.dynamic_slice_in_dim(skip, core * half, half, 0)
    gated = (gate * (long_conv.astype(jnp.float32) + own_skip[:, None] * source)).astype(BF)
    gated = gated.reshape(half, 2, rows).transpose(1, 0, 2)
    gated = jnp.broadcast_to(gated, (tp_count,) + gated.shape).reshape(-1, half, rows)
    gated = exchange(gated, ("seq", "tp"), column_groups).reshape(-1, rows)
    out = lax.dot_general(
        gated, wanted, (((0,), (0,)), ((), ())), preferred_element_type=jnp.float32
    )
    return out.astype(BF)


def solution(mesh):
    width, depth, tp = 4, 8, mesh.shape["tp"]
    place = lambda x, z, c: (x * depth + z) * 2 + c
    chips = [(x, z) for x in range(width) for z in range(depth)]
    x_groups = [[place(x, z, c) for x in range(width)] for z in range(depth) for c in range(2)]
    zc_groups = [[place(x, z, c) for z in range(depth) for c in range(2)] for x in range(width)]
    chip_groups = [[place(x, z, c) for x, z in chips] for c in range(2)]
    column_groups = [
        [place(x, z, c) * tp + y for y in range(tp) for c in range(2)] for x, z in chips
    ]
    return jax.shard_map(
        functools.partial(body, (x_groups, zc_groups, chip_groups, column_groups)),
        mesh=mesh,
        in_specs=(
            P("seq", "tp"),
            P(None, "seq", "tp"),
            P(None, None, "tp"),
            P("seq", "tp"),
            P("tp"),
            P("tp", None),
        ),
        out_specs=P("seq", "tp"),
        check_vma=False,
    )
```
